32 devices in a mesh: seq: 4 (over y, core), dp: 8 (over z, x).
Axes of the slice: x: 2, y: 2, z: 4, core: 2. Of those that a mesh axis runs over, the one named last changes fastest.
Arguments:
- tokens: bfloat16 [8, 2048, 1024], P('dp', 'seq'), may hold values from -6 to 6
- cotangent: bfloat16 [8, 2048, 1024], P('dp', 'seq'), may hold values from -6 to 6
- segments: int32 [8, 2048], P('dp'), may hold values from 0 to 2047, as said below
- routes: int32 [8, 2048, 8], P('dp', 'seq'), may hold values from 0 to 15, all different within a row; in each aligned block of 512 rows (0 to 511, 512 to 1023, ..., all dimensions but the last counted through in order) at most 320 rows name the same one
- w_qkv: bfloat16 [1024, 2048], P(None, ('seq', 'dp')), may hold values from -0.25 to 0.25
- w_out: bfloat16 [1024, 1024], P(None, ('seq', 'dp')), may hold values from -1 to 1
- norm_gains: bfloat16 [2, 1024], P(None, ('seq', 'dp')), may hold values from 0.5 to 1.5
- router: bfloat16 [16, 1024], P(None, ('seq', 'dp')), may hold values from -0.09375 to 0.09375
- w_gate_up: bfloat16 [16, 1024, 1024], P(None, None, ('seq', 'dp')), may hold values from -0.1875 to 0.1875
- w_down: bfloat16 [16, 512, 1024], P(None, None, ('seq', 'dp')), may hold values from -1.5 to 1.5
Outputs:
- mixed: bfloat16 [8, 2048, 1024], P('dp', 'seq')
- input_grad: float32 [8, 2048, 1024], P('dp', 'seq')
- grad_qkv: float32 [1024, 2048], P(None, ('seq', 'dp'))
- grad_out: float32 [1024, 1024], P(None, ('seq', 'dp'))
- grad_gains: float32 [2, 1024], P(None, ('seq', 'dp'))
- grad_router: float32 [16, 1024], P(None, ('seq', 'dp'))
- grad_gate_up: float32 [16, 1024, 1024], P(None, None, ('seq', 'dp'))
- grad_down: float32 [16, 512, 1024], P(None, None, ('seq', 'dp'))
The draws below stay inside these ranges and needn't reach their ends.
Inputs may be any that keep to these rules, and one draw needn't show every extreme that they name: segments[b, i] is the index of the first token of the document holding token i; it never decreases along a sequence and starts at 0. `routes`: each token names 8 different experts; within each aligned block of 512 tokens of a sequence no expert is named by more than 320 tokens, and in some block one is named by exactly 320.
All inputs are finite; a program needn't handle non-finite values.
Results may differ from the reference program's by a relative error of at most 0.017.
The reference program's roundings to bfloat16 on the way count: a program that leaves them out, or rounds other values in their place, can miss the bound.
Values may be sent and summed in bfloat16 or wider, within the bound.
A program may use at most 384 MiB of HBM per device.

```python
import math
import jax
import jax.numpy as jnp
import numpy as np
from jax import lax

D = 1024
HEADS = 16
KV_HEADS = 8
HEAD_DIM = 64
FF = 512
TOP = 8
EXPERTS = 16
TOK_DEV = 512
LENGTH = 2048
SEQUENCES = 8
QKV = 2048
CAP = 320


def draw_segments(key, part):
    key = jax.random.fold_in(key, 11)
    key_flags, key_first, key_last = jax.random.split(key, 3)
    index = jnp.arange(LENGTH, dtype=jnp.int32)[None, :]
    flags = jax.random.randint(key_flags, (SEQUENCES, LENGTH), 0, max(LENGTH // 16, 2)) == 0
    first = jax.random.randint(key_first, (SEQUENCES, 1), 1, max(LENGTH // 8, 2))
    last = jax.random.randint(key_last, (SEQUENCES, 1), LENGTH - LENGTH // 8, LENGTH)
    flags = jnp.where((index > first) & (index < last), False, flags)
    flags = flags | (index == first) | (index == last) | (index == 0)
    starts = jnp.where(flags, index, 0).astype(jnp.int32)
    return lax.cummax(starts, axis=1)


def block_scale(own_key, shape, cuts, least, largest):
    level = 1.0
    for axis_at, shards_of in cuts:
        heights = jax.random.uniform(jax.random.fold_in(jax.random.fold_in(own_key, 6), axis_at), (shards_of,), jnp.float32, least / len(cuts), largest / len(cuts))
        level = level * jnp.repeat(jnp.exp(heights), shape[axis_at] // shards_of).reshape((-1,) + (1,) * (len(shape) - 1 - axis_at))
    return level


def assign_block(own_key, own, number, rows, amount, top, bound, skew):
    sequence = jax.random.permutation(own_key, amount)
    heavy_load, ordinary = portions_of(amount, rows * top, bound, skew, True), portions_of(amount, rows * top, bound, skew, False)
    places = jnp.arange(amount)

    def named(tallies, turn):
        used = int((tallies > 0).sum())
        fixed = max(1, used // 4)
        passed = fixed + (places - fixed + turn * (used - fixed)) % max(1, amount - fixed)
        return jnp.zeros((amount,), jnp.int32).at[sequence[jnp.where(places < fixed, places, passed)]].set(jnp.asarray(tallies, jnp.int32))

    tallies = jnp.where(number % 4 == 0, named(heavy_load, number // 4), named(ordinary, number - number // 4 - 1))
    mixed = jax.random.permutation(jax.random.fold_in(own, 3), amount)
    source_of, receiver = mixed[0:amount // 2 * 2:2], mixed[1:amount // 2 * 2:2]
    room = jnp.minimum(tallies[source_of] - 1, bound - tallies[receiver]) // 2
    room = jnp.where((source_of == sequence[0]) | (receiver == sequence[0]) | (tallies[receiver] == 0), 0, jnp.maximum(room, 0))
    passed = jax.random.randint(jax.random.fold_in(own, 4), (amount // 2,), 0, 1 << 20) % (room + 1)
    tallies = tallies.at[source_of].add(-passed).at[receiver].add(passed)
    items = jnp.searchsorted(jnp.cumsum(tallies), jnp.arange(rows * top), side="right").astype(jnp.int32)
    listing = items.reshape(top, rows).T
    listing = listing[jax.random.permutation(jax.random.fold_in(own, 1), rows)]
    turn = jax.random.randint(jax.random.fold_in(own, 2), (rows, 1), 0, top)
    return jnp.take_along_axis(listing, (jnp.arange(top)[None, :] + turn) % top, axis=1)


def portions_of(amount, total, most, slope, full):
    portions = [(1 << 20) // math.isqrt(rank ** slope) + 1 for rank in range(1, amount + 1)]
    largest = most if full else min(most, max(-(-total // amount), total * portions[0] // sum(portions)))
    least = 1 if total - largest >= amount - 1 else 0
    holding, spare = [largest] + [least] * (amount - 1), total - largest - least * (amount - 1)
    while spare > 0:
        movable = [i for i in range(1, amount) if holding[i] < largest] or [i for i in range(1, amount) if holding[i] < most]
        mass, left = sum([portions[i] for i in movable]), spare
        for i in movable:
            addition = min(most - holding[i], max(1, left * portions[i] // mass), spare)
            holding[i] = holding[i] + addition
            spare = spare - addition
    return np.array(holding)


def gaussian(own_key, extent, scale, most, shards=(), kind=jnp.bfloat16):
    result = jax.random.normal(own_key, extent, jnp.float32) * scale
    if len(shards) > 0:
        result = block_scale(own_key, extent, shards, -0.22, 0.18) * result
    return jnp.clip(result, min=-most, max=most).astype(kind)


def setup_inputs(seed: int = 0) -> dict:
    streams_of = jax.random.split(jax.random.key(seed), 11)
    tokens = gaussian(streams_of[0], (SEQUENCES, LENGTH, D), 1.0, 6.0, ((0, 8), (1, 4)))
    cotangent = gaussian(streams_of[1], (SEQUENCES, LENGTH, D), 1.0, 6.0, ((0, 8), (1, 4)))
    segments = draw_segments(jax.random.fold_in(streams_of[10], 71), 0)
    routes_keys = jax.random.split(jax.random.fold_in(streams_of[3], 1), SEQUENCES * LENGTH // TOK_DEV)
    routes_turns = jax.random.permutation(jax.random.fold_in(streams_of[3], 3), SEQUENCES * LENGTH // TOK_DEV)
    routes = jax.vmap(lambda own, number: assign_block(jax.random.fold_in(streams_of[3], 2), own, number, TOK_DEV, EXPERTS, TOP, CAP, 1))(routes_keys, routes_turns).reshape((SEQUENCES, LENGTH, TOP))
    w_qkv = gaussian(streams_of[4], (D, QKV), (D // 2) ** -0.5, 0.25, ((1, 32),))
    w_out = gaussian(streams_of[5], (HEADS * HEAD_DIM, D), (HEADS * HEAD_DIM // 32) ** -0.5, 1.0, ((1, 32),))
    norm_gains = jnp.clip(1.0 + 0.1 * jax.random.normal(streams_of[6], (2, D), jnp.float32), 0.5, 1.5).astype(jnp.bfloat16)
    router = gaussian(streams_of[7], (EXPERTS, D), (4 * D) ** -0.5, 0.09375, ((1, 32),))
    w_gate_up = gaussian(streams_of[8], (EXPERTS, D, 2 * FF), D ** -0.5, 0.1875, ((2, 32),))
    w_down = gaussian(streams_of[9], (EXPERTS, FF, D), (FF // 32) ** -0.5, 1.5, ((2, 32),))
    return {"tokens": tokens, "cotangent": cotangent, "segments": segments, "routes": routes, "w_qkv": w_qkv, "w_out": w_out, "norm_gains": norm_gains, "router": router, "w_gate_up": w_gate_up, "w_down": w_down}


NORM_EPSILON = 1e-06
ROPE_THETA = 10000.0
HIGHEST = lax.Precision.HIGHEST

@jax.custom_vjp
def low(v):
    return lax.optimization_barrier(v.astype(jnp.bfloat16)).astype(jnp.float32)

@jax.custom_vjp
def low_back(v):
    return v

def low_keep(v):
    return (low(v), None)

def low_pass(kept, grad):
    return (grad,)

def back_keep(v):
    return (v, None)

def back_low(kept, grad):
    return (low(grad),)
low.defvjp(low_keep, low_pass)
low_back.defvjp(back_keep, back_low)

def rms_scale(tensor):
    return lax.rsqrt(lax.optimization_barrier(jnp.mean(tensor * tensor, axis=-1, keepdims=True)) + NORM_EPSILON)

def rotate(tensor, positions, direction):
    half_dim = tensor.shape[-1] // 2
    frequency = ROPE_THETA ** (-jnp.arange(half_dim, dtype=jnp.float32) / half_dim)
    angles = positions.astype(jnp.float32)[:, None] * frequency[None, :]
    cosine = jnp.cos(angles)[:, None, :]
    sine_part = direction * jnp.sin(angles)[:, None, :]
    first_half = tensor[..., :half_dim]
    second_half = tensor[..., half_dim:]
    return jnp.concatenate([first_half * cosine - second_half * sine_part, second_half * cosine + first_half * sine_part], axis=-1)

def route_tables(route_rows, expert_count, capacity):
    pair_count = route_rows.shape[0] * route_rows.shape[1]
    flat_routes = route_rows.reshape(pair_count).astype(jnp.int32)
    expert_hits = (flat_routes[:, None] == jnp.arange(expert_count, dtype=jnp.int32)[None, :]).astype(jnp.int32)
    running = jnp.cumsum(expert_hits, axis=0, dtype=jnp.int32) - 1
    within = lax.optimization_barrier(jnp.sum(running * expert_hits, axis=1, dtype=jnp.int32))
    slot_of_pair = (flat_routes * capacity + within).astype(jnp.int32)
    slot_table = jnp.full((expert_count * capacity,), pair_count, dtype=jnp.int32)
    slot_table = slot_table.at[slot_of_pair].set(jnp.arange(pair_count, dtype=jnp.int32))
    return (slot_of_pair, slot_table)

def expert_block(block_input, block_logits, route_rows, gate_up, down_proj):
    row_count = block_input.shape[0]
    feature_count = block_input.shape[1]
    matches = route_rows[:, :, None] == jnp.arange(EXPERTS, dtype=jnp.int32)[None, None, :]
    chosen = lax.optimization_barrier(jnp.sum(jnp.where(matches, block_logits[:, None, :], 0.0), axis=-1))
    gate_values = jax.nn.softmax(chosen, axis=-1)
    slot_of_pair, slot_table = route_tables(route_rows, EXPERTS, CAP)
    token_of_slot = (slot_table // TOP).astype(jnp.int32)
    padded = jnp.concatenate([block_input, jnp.zeros((1, feature_count), block_input.dtype)], axis=0)
    expert_input = padded[token_of_slot].reshape(EXPERTS, CAP, feature_count)
    gate_up_out = low_back(jnp.einsum('ecd,edf->ecf', expert_input, gate_up, precision=HIGHEST))
    swiglu_out = low(jax.nn.silu(gate_up_out[..., :FF]) * gate_up_out[..., FF:])
    expert_out = low_back(jnp.einsum('ecf,efd->ecd', swiglu_out, down_proj, precision=HIGHEST))
    gate_flat = jnp.concatenate([gate_values.reshape(row_count * TOP), jnp.zeros((1,), gate_values.dtype)])
    slot_gates = gate_flat[slot_table].reshape(EXPERTS, CAP, 1)
    weighted = (expert_out * slot_gates).reshape(EXPERTS * CAP, feature_count)
    return jax.ops.segment_sum(weighted, token_of_slot, num_segments=row_count + 1)[:row_count]

def attend(query_group, key_head, value_head, key_mask):
    scores = low_back(jnp.einsum('qgd,kd->gqk', query_group, key_head, precision=HIGHEST) * HEAD_DIM ** (-0.5))
    scores = jnp.where(key_mask[None], scores, -1e+30)
    softmax_weights = jax.nn.softmax(scores, axis=-1)
    return jnp.einsum('gqk,kd->qgd', low(softmax_weights), value_head, precision=HIGHEST)

def sequence_layer(inputs, segment_ids, route_rows, qkv_proj, out_proj, norm_gain, router_proj, gate_up, down_proj):
    length = inputs.shape[0]
    position = jnp.arange(length, dtype=jnp.int32)
    rotary = position - segment_ids
    key_mask = (position[None, :] <= position[:, None]) & (segment_ids[None, :] == segment_ids[:, None])
    first_hidden = low(inputs * rms_scale(inputs) * norm_gain[0])
    projected = low_back(jnp.dot(first_hidden, qkv_proj, precision=HIGHEST))
    query_width = HEADS * HEAD_DIM
    key_width = KV_HEADS * HEAD_DIM
    group_size = HEADS // KV_HEADS
    queries = low(rotate(projected[:, :query_width].reshape(length, HEADS, HEAD_DIM), rotary, 1.0))
    key_rows = low(rotate(projected[:, query_width:query_width + key_width].reshape(length, KV_HEADS, HEAD_DIM), rotary, 1.0))
    value_rows = low(projected[:, query_width + key_width:].reshape(length, KV_HEADS, HEAD_DIM))
    query_heads = queries.reshape(length, KV_HEADS, group_size, HEAD_DIM).transpose(1, 0, 2, 3)

    def one_head(operands):
        return attend(operands[0], operands[1], operands[2], key_mask)
    attended = lax.map(jax.checkpoint(one_head), (query_heads, key_rows.transpose(1, 0, 2), value_rows.transpose(1, 0, 2)))
    attended = low(low_back(attended.transpose(1, 0, 2, 3).reshape(length, query_width)))
    residual = inputs + low_back(jnp.dot(attended, out_proj, precision=HIGHEST))
    second_hidden = low(residual * rms_scale(residual) * norm_gain[1])
    logits = low_back(jnp.dot(second_hidden, router_proj.T, precision=HIGHEST))
    mixture = jax.vmap(expert_block, in_axes=(0, 0, 0, None, None))(second_hidden.reshape(-1, TOK_DEV, D), logits.reshape(-1, TOK_DEV, EXPERTS), route_rows.reshape(-1, TOK_DEV, TOP), gate_up, down_proj)
    return residual + mixture.reshape(length, D)

def reference(tokens, cotangent, segments, routes, w_qkv, w_out, norm_gains, router, w_gate_up, w_down):
    weights = tuple((tensor.astype(jnp.float32) for tensor in (w_qkv, w_out, norm_gains, router, w_gate_up, w_down)))

    def forward(layer_input, params):

        def one_sequence(operands):
            return sequence_layer(operands[0], operands[1], operands[2], params[0], params[1], params[2], params[3], params[4], params[5])
        return lax.map(jax.checkpoint(one_sequence), (layer_input, segments, routes))
    outputs, pullback = jax.vjp(forward, tokens.astype(jnp.float32), weights)
    input_grad, weight_grads = pullback(cotangent.astype(jnp.float32))
    return (outputs.astype(jnp.bfloat16), input_grad, weight_grads[0], weight_grads[1], weight_grads[2], weight_grads[3], weight_grads[4], weight_grads[5])
```

```python
import functools

import jax
import jax.numpy as jnp
from jax import lax
from jax.sharding import PartitionSpec as P

HEADS = 16
KV_HEADS = 8
HEAD_DIM = 64
FF = 512
EXPERTS = 16


NORM_EPSILON = 1e-06
ROPE_THETA = 10000.0


def rms_scale(tensor):
    return lax.rsqrt(jnp.mean(tensor * tensor, axis=-1, keepdims=True) + NORM_EPSILON)


def rotate(tensor, positions, direction):
    half_dim = tensor.shape[-1] // 2
    frequency = ROPE_THETA ** (-jnp.arange(half_dim, dtype=jnp.float32) / half_dim)
    angles = positions.astype(jnp.float32)[:, None] * frequency[None, :]
    cosine = jnp.cos(angles)[:, None, :]
    sine_part = direction * jnp.sin(angles)[:, None, :]
    first_half = tensor[..., :half_dim]
    second_half = tensor[..., half_dim:]
    return jnp.concatenate(
        [
            first_half * cosine - second_half * sine_part,
            second_half * cosine + first_half * sine_part,
        ],
        axis=-1,
    )


def ring_sum(parts, axis, size, dtype):
    if size == 1:
        return parts[0].astype(jnp.float32)
    if size > 16:
        return lax.psum_scatter(parts.astype(dtype), axis, scatter_dimension=0).astype(jnp.float32)
    order = list(range(0, size, 2)) + list(range(size - 1 - size % 2, 0, -2))
    place_of = [0] * size
    for place, owner in enumerate(order):
        place_of[owner] = place
    place = jnp.asarray(place_of, jnp.int32)[lax.axis_index(axis)]
    owners = jnp.asarray(order, jnp.int32)
    ahead = [(order[i], order[(i + 1) % size]) for i in range(size)]
    back = [(after, before) for before, after in ahead]
    half = parts.shape[1] // 2

    def piece(where, first):
        owner = owners[lax.rem(where + 4 * size, size)]
        block = lax.dynamic_slice_in_dim(parts, owner, 1, 0)[0]
        return (block[:half] if first else block[half:]).astype(jnp.float32)

    up = piece(place - 1, True)
    down = piece(place + 1, False)
    for step in range(1, size):
        up = lax.ppermute(up.astype(dtype), axis, ahead)
        down = lax.ppermute(down.astype(dtype), axis, back)
        up = up.astype(jnp.float32) + piece(place - 1 - step, True)
        down = down.astype(jnp.float32) + piece(place + 1 + step, False)
    return jnp.concatenate([up, down], axis=0)


def seq_sum(parts, dtype):
    moved = lax.all_to_all(parts.astype(dtype), "seq", 0, 0, tiled=True)
    return jnp.sum(moved.astype(jnp.float32), axis=0)


def per_device(
    seq_size, dp_size, tokens, cotangent, segments, routes, w_qkv, w_out, norm_gains, router, w_gate_up, w_down
):
    bf16 = jnp.bfloat16
    devices = seq_size * dp_size
    own_experts = EXPERTS // seq_size
    width = w_qkv.shape[0]
    qkv_cols, out_cols, small_cols = w_qkv.shape[1], w_out.shape[1], router.shape[1]
    small_rows = 2 + EXPERTS
    dense_rows = qkv_cols + out_cols
    packed_rows = -(-(dense_rows + 1) // 32) * 32

    def pack(qkv_part, out_part, small_part):
        blocks = qkv_part.shape[0]
        flat = small_part.reshape(blocks, 1, small_rows * small_cols)
        flat = jnp.pad(
            flat,
            ((0, 0), (0, packed_rows - dense_rows - 1), (0, width - small_rows * small_cols)),
        )
        return jnp.concatenate([qkv_part, out_part, flat], axis=1)

    packed = pack(
        w_qkv.T[None], w_out.T[None], jnp.concatenate([norm_gains, router], axis=0)[None]
    )[0]
    packed_full = lax.all_gather(packed, ("seq", "dp"), axis=0, tiled=False)
    qkv_t = packed_full[:, :qkv_cols].reshape(devices * qkv_cols, width)
    out_t = packed_full[:, qkv_cols:dense_rows].reshape(devices * out_cols, width)
    small = (
        packed_full[:, dense_rows, : small_rows * small_cols]
        .reshape(devices, small_rows, small_cols)
        .transpose(1, 0, 2)
        .reshape(small_rows, devices * small_cols)
    )
    gain_rows, router_proj = small[:2], small[2:]

    def own_weights(weight):
        depth, columns = weight.shape[1], weight.shape[2]
        turned = weight.transpose(0, 2, 1).reshape(seq_size, own_experts, columns, depth)
        moved = lax.all_to_all(turned, "seq", 0, 0, tiled=True).transpose(1, 0, 2, 3)
        whole = lax.all_gather(moved, "dp", axis=2, tiled=True)
        return whole.reshape(own_experts, devices * columns, depth)

    gate_up_t = own_weights(w_gate_up)
    down_t = own_weights(w_down)
    routes_seq = lax.all_gather(routes[0], "seq", axis=0, tiled=True)
    dy_seq = lax.all_gather(cotangent[0], "seq", axis=0, tiled=True)
    norm_gain = gain_rows.astype(jnp.float32)
    inputs = tokens[0].astype(jnp.float32)
    row_count = inputs.shape[0]
    feature_count = inputs.shape[1]
    length = segments.shape[1]
    score_scale = HEAD_DIM ** (-0.5)
    query_width = HEADS * HEAD_DIM
    key_width = KV_HEADS * HEAD_DIM
    group_size = HEADS // KV_HEADS
    row_start = lax.axis_index("seq") * row_count
    own_index = row_start + jnp.arange(row_count, dtype=jnp.int32)
    segment_row = segments[0]
    own_segment = lax.dynamic_slice_in_dim(segment_row, row_start, row_count)
    rotary = own_index - own_segment
    key_index = jnp.arange(length, dtype=jnp.int32)
    key_mask = (key_index[None, :] <= own_index[:, None]) & (
        segment_row[None, :] == own_segment[:, None]
    )
    first_scale = rms_scale(inputs)
    first_normed = inputs * first_scale
    first_hidden = (first_normed * norm_gain[0]).astype(jnp.bfloat16)
    projected = lax.dot_general(
        first_hidden, qkv_t, (((1,), (1,)), ((), ())), preferred_element_type=jnp.float32
    )
    queries = rotate(
        projected[:, :query_width].reshape(row_count, HEADS, HEAD_DIM), rotary, 1.0
    ).astype(jnp.bfloat16)
    key_rows = rotate(
        projected[:, query_width : query_width + key_width].reshape(row_count, KV_HEADS, HEAD_DIM),
        rotary,
        1.0,
    ).astype(jnp.bfloat16)
    value_rows = projected[:, query_width + key_width :].astype(jnp.bfloat16)
    outgoing = jnp.concatenate([key_rows.reshape(row_count, key_width), value_rows], axis=1)
    sequence_kv = lax.all_gather(outgoing, "seq", axis=0, tiled=True)
    keys_all = sequence_kv[:, :key_width].reshape(length, KV_HEADS, HEAD_DIM).transpose(1, 0, 2)
    values_all = sequence_kv[:, key_width:].reshape(length, KV_HEADS, HEAD_DIM).transpose(1, 0, 2)
    query_heads = queries.reshape(row_count, KV_HEADS, group_size, HEAD_DIM).transpose(1, 0, 2, 3)

    def head_scores(query_group, key_head):
        scores = (
            jnp.einsum("qgd,kd->gqk", query_group, key_head, preferred_element_type=jnp.float32)
            * score_scale
        )
        return jnp.where(key_mask[None], scores, -1e30)

    def forward_head(operands):
        query_group, key_head, value_head = operands
        scores = head_scores(query_group, key_head)
        row_peak = jnp.max(scores, axis=-1, keepdims=True)
        shifted = jnp.exp(scores - row_peak)
        row_total = jnp.sum(shifted, axis=-1, keepdims=True)
        softmax_weights = (shifted / row_total).astype(jnp.bfloat16)
        attended_head = jnp.einsum(
            "gqk,kd->qgd", softmax_weights, value_head, preferred_element_type=jnp.float32
        )
        return (attended_head.astype(jnp.bfloat16), (row_peak + jnp.log(row_total))[..., 0])

    attended_heads, log_totals = lax.map(forward_head, (query_heads, keys_all, values_all))
    attended = attended_heads.transpose(1, 0, 2, 3).reshape(row_count, query_width)
    residual = inputs + lax.dot_general(
        attended, out_t, (((1,), (1,)), ((), ())), preferred_element_type=jnp.float32
    )
    second_scale = rms_scale(residual)
    second_normed = residual * second_scale
    second_hidden = (second_normed * norm_gain[1]).astype(jnp.bfloat16)
    first_expert = lax.axis_index("seq") * own_experts
    hidden_seq = lax.all_gather(second_hidden, "seq", axis=0, tiled=True)

    def dense_gates(hidden, route_rows):
        logits = lax.dot_general(
            hidden, router_proj, (((1,), (1,)), ((), ())), preferred_element_type=jnp.float32
        )
        used = jnp.any(
            route_rows[:, :, None] == jnp.arange(EXPERTS, dtype=jnp.int32)[None, None, :], axis=1
        )
        kept = jnp.where(used, logits, -jnp.inf)
        shifted = jnp.exp(kept - jnp.max(kept, axis=-1, keepdims=True))
        return used, shifted / jnp.sum(shifted, axis=-1, keepdims=True)

    used, gates = dense_gates(second_hidden, routes[0])
    gates_seq = dense_gates(hidden_seq, routes_seq)[1]
    own_gates = lax.dynamic_slice_in_dim(gates_seq, first_expert, own_experts, 1)[:, :, None]
    inner = own_experts * FF
    gu = lax.dot_general(
        hidden_seq,
        gate_up_t.reshape(own_experts * 2 * FF, width),
        (((1,), (1,)), ((), ())),
        preferred_element_type=jnp.float32,
    ).reshape(length, own_experts, 2 * FF)
    gate_part = gu[..., :FF]
    up_part = gu[..., FF:]
    sigmoid_gate = jax.nn.sigmoid(gate_part)
    silu_gate = gate_part * sigmoid_gate
    act = (silu_gate * up_part).astype(bf16).astype(jnp.float32)
    act_gated = (act * own_gates).astype(bf16).reshape(length, inner)
    down_flat = down_t.transpose(1, 0, 2).reshape(width, inner)
    mixture_part = lax.dot_general(
        act_gated, down_flat, (((1,), (1,)), ((), ())), preferred_element_type=jnp.float32
    )
    grad_inner = jnp.dot(dy_seq, down_flat, preferred_element_type=jnp.float32).reshape(
        length, own_experts, FF
    )
    grad_gates_part = jnp.sum(act * grad_inner, axis=-1)
    grad_act = grad_inner * own_gates
    silu_slope = sigmoid_gate * (1.0 + gate_part * (1.0 - sigmoid_gate))
    grad_gu = (
        jnp.concatenate([grad_act * up_part * silu_slope, grad_act * silu_gate], axis=-1)
        .astype(bf16)
        .reshape(length, own_experts * 2 * FF)
    )
    grad_hidden_part = jnp.dot(
        grad_gu,
        gate_up_t.reshape(own_experts * 2 * FF, width),
        preferred_element_type=jnp.float32,
    )
    high = grad_gates_part.astype(bf16)
    low = (grad_gates_part - high.astype(jnp.float32)).astype(bf16)
    extra = jnp.pad(jnp.concatenate([high, low], axis=1), ((0, 0), (0, 128 - 2 * own_experts)))
    payload = jnp.concatenate([grad_hidden_part.astype(bf16), extra], axis=1)
    moved = lax.all_to_all(
        payload.reshape(seq_size, row_count, width + 128), "seq", 0, 0, tiled=True
    )
    grad_second = jnp.sum(moved[:, :, :width].astype(jnp.float32), axis=0)
    parts = moved[:, :, width : width + 2 * own_experts].astype(jnp.float32)
    grad_gates = (
        (parts[..., :own_experts] + parts[..., own_experts:])
        .transpose(1, 0, 2)
        .reshape(row_count, EXPERTS)
    )
    grad_output = cotangent[0].astype(jnp.float32)
    grad_logits = jnp.where(
        used,
        gates * (grad_gates - jnp.sum(gates * grad_gates, axis=-1, keepdims=True)),
        0.0,
    ).astype(bf16)
    grad_second = grad_second + jnp.dot(
        grad_logits, router_proj, preferred_element_type=jnp.float32
    )
    mixture = seq_sum(mixture_part.reshape(seq_size, row_count, width), bf16)
    mixed = (residual + mixture).astype(bf16)[None]

    def expert_owned(local):
        columns, depth = local.shape[1] // devices, local.shape[2]
        blocks = (
            local.astype(bf16)
            .reshape(own_experts, seq_size, dp_size, columns, depth)
            .transpose(2, 1, 0, 3, 4)
            .reshape(dp_size, seq_size * own_experts, columns, depth)
        )
        mine = ring_sum(blocks, "dp", dp_size, bf16)
        mine = mine.reshape(seq_size, own_experts, columns, depth)
        sent = lax.all_to_all(mine.astype(bf16), "seq", 0, 0, tiled=True)
        return (
            sent.reshape(EXPERTS, columns, depth).transpose(0, 2, 1).astype(jnp.float32)
        )

    grad_gate_up_local = lax.dot_general(
        grad_gu, hidden_seq, (((0,), (0,)), ((), ())), preferred_element_type=jnp.float32
    ).reshape(own_experts, 2 * FF, width)
    grad_gate_up = expert_owned(grad_gate_up_local)
    grad_down_local = (
        lax.dot_general(
            dy_seq, act_gated, (((0,), (0,)), ((), ())), preferred_element_type=jnp.float32
        )
        .astype(bf16)
        .reshape(width, own_experts, FF)
        .transpose(1, 0, 2)
    )
    grad_down = expert_owned(grad_down_local)
    grad_router_local = lax.dot_general(
        grad_logits, second_hidden, (((0,), (0,)), ((), ())), preferred_element_type=jnp.float32
    )
    gain_two = jnp.sum(grad_second * second_normed, axis=0)
    grad_normed_two = grad_second * norm_gain[1]
    grad_residual = grad_output + second_scale * (
        grad_normed_two
        - second_normed * jnp.mean(grad_normed_two * second_normed, axis=-1, keepdims=True)
    )
    grad_branch = grad_residual.astype(jnp.bfloat16)
    grad_attended = lax.dot_general(
        grad_branch, out_t, (((1,), (0,)), ((), ())), preferred_element_type=jnp.float32
    ).astype(jnp.bfloat16)
    grad_out_local = lax.dot_general(
        grad_branch, attended, (((0,), (0,)), ((), ())), preferred_element_type=jnp.float32
    )
    grad_heads = grad_attended.reshape(row_count, KV_HEADS, group_size, HEAD_DIM).transpose(
        1, 0, 2, 3
    )

    def backward_head(operands):
        query_group, key_head, value_head, grad_group, log_total = operands
        scores = head_scores(query_group, key_head)
        softmax_full = jnp.exp(scores - log_total[..., None])
        grad_weights = jnp.einsum(
            "qgd,kd->gqk", grad_group, value_head, preferred_element_type=jnp.float32
        )
        row_delta = jnp.sum(softmax_full * grad_weights, axis=-1, keepdims=True)
        grad_scores = (softmax_full * (grad_weights - row_delta)).astype(jnp.bfloat16)
        grad_query = (
            jnp.einsum("gqk,kd->qgd", grad_scores, key_head, preferred_element_type=jnp.float32)
            * score_scale
        )
        grad_key = (
            jnp.einsum("gqk,qgd->kd", grad_scores, query_group, preferred_element_type=jnp.float32)
            * score_scale
        )
        grad_value = jnp.einsum(
            "gqk,qgd->kd",
            softmax_full.astype(jnp.bfloat16),
            grad_group,
            preferred_element_type=jnp.float32,
        )
        return (grad_query, grad_key, grad_value)

    query_grads, key_grads, value_grads = lax.map(
        backward_head, (query_heads, keys_all, values_all, grad_heads, log_totals)
    )
    key_terms = jnp.concatenate(
        [
            key_grads.transpose(1, 0, 2).reshape(length, key_width),
            value_grads.transpose(1, 0, 2).reshape(length, key_width),
        ],
        axis=1,
    )
    key_owned = seq_sum(key_terms.reshape(seq_size, row_count, 2 * key_width), bf16)
    grad_query_rows = rotate(
        query_grads.transpose(1, 0, 2, 3).reshape(row_count, HEADS, HEAD_DIM), rotary, -1.0
    ).reshape(row_count, query_width)
    grad_key_rows = rotate(
        key_owned[:, :key_width].reshape(row_count, KV_HEADS, HEAD_DIM), rotary, -1.0
    ).reshape(row_count, key_width)
    grad_projected = jnp.concatenate(
        [grad_query_rows, grad_key_rows, key_owned[:, key_width:]], axis=1
    ).astype(jnp.bfloat16)
    grad_first = lax.dot_general(
        grad_projected, qkv_t, (((1,), (0,)), ((), ())), preferred_element_type=jnp.float32
    )
    grad_qkv_local = lax.dot_general(
        grad_projected, first_hidden, (((0,), (0,)), ((), ())), preferred_element_type=jnp.float32
    )
    gain_one = jnp.sum(grad_first * first_normed, axis=0)
    grad_normed_one = grad_first * norm_gain[0]
    input_grad = grad_residual + first_scale * (
        grad_normed_one
        - first_normed * jnp.mean(grad_normed_one * first_normed, axis=-1, keepdims=True)
    )
    small_grads = (
        jnp.concatenate([gain_one[None], gain_two[None], grad_router_local], axis=0)
        .reshape(small_rows, devices, small_cols)
        .transpose(1, 0, 2)
    )
    dense_grads = pack(
        grad_qkv_local.astype(bf16).reshape(devices, qkv_cols, width),
        grad_out_local.astype(bf16).reshape(devices, out_cols, width),
        small_grads.astype(bf16),
    ).reshape(seq_size, dp_size, packed_rows, width)
    dense_owned = ring_sum(seq_sum(dense_grads, bf16), "dp", dp_size, bf16)
    small_owned = dense_owned[dense_rows, : small_rows * small_cols].reshape(
        small_rows, small_cols
    )
    return (
        mixed,
        input_grad[None],
        dense_owned[:qkv_cols].T,
        dense_owned[qkv_cols:dense_rows].T,
        small_owned[:2],
        small_owned[2:],
        grad_gate_up,
        grad_down,
    )


def solution(mesh):
    placed = (
        P("dp", "seq", None),
        P("dp", "seq", None),
        P("dp", None),
        P("dp", "seq", None),
        P(None, ("seq", "dp")),
        P(None, ("seq", "dp")),
        P(None, ("seq", "dp")),
        P(None, ("seq", "dp")),
        P(None, None, ("seq", "dp")),
        P(None, None, ("seq", "dp")),
    )
    return jax.shard_map(
        functools.partial(per_device, mesh.shape["seq"], mesh.shape["dp"]),
        mesh=mesh,
        in_specs=placed,
        out_specs=(
            P("dp", "seq", None),
            P("dp", "seq", None),
            P(None, ("seq", "dp")),
            P(None, ("seq", "dp")),
            P(None, ("seq", "dp")),
            P(None, ("seq", "dp")),
            P(None, None, ("seq", "dp")),
            P(None, None, ("seq", "dp")),
        ),
        check_vma=False,
    )
```
